128 devices in a mesh: aux: 4 (over y), orb: 32 (over x, z, core).
Axes of the slice: x: 4, y: 4, z: 4, core: 2. Of those that a mesh axis runs over, the one named last changes fastest.
Arguments:
- half_blocks: bfloat16 [8, 32, 128, 2, 128, 128], P('aux', 'orb'), may hold values from -6 to 6
- fit_coeffs: bfloat16 [8, 8], replicated, may hold values from -2 to 2
- pair_map: int32 [32, 128, 2, 2], replicated, may hold values from 0 to 383, as said below
- block_owner: int32 [384, 2], replicated, may hold values from 0 to 127, as said below
- slot_counts: int32 [32, 128], replicated, may hold values from 1 to 2, as said below
Outputs:
- exchange: float32 [2048, 2048], P(('aux', 'orb'))
The draws below stay inside these ranges and needn't reach their ends.
Inputs may be any that keep to these rules, and one draw needn't show every extreme that they name: pair_map[o, d, s, 0] is a row block below 16; pair_map[o, d, s, 1] is an orbital block owned by device d; pairs may repeat. `block_owner`: every device owns exactly 3 orbital blocks, with local indices 0 to 2. `slot_counts`: some owner device receives 2 live slots from every source orbital index.
All inputs are finite; a program needn't handle non-finite values.
Results may differ from the reference program's by a relative error of at most 0.00051.
Values may be sent and summed in bfloat16 or wider, within the bound.
A program may use at most 128 MiB of HBM per device.

```python
import math
import jax
import jax.numpy as jnp
from jax import lax

BS = 128
OBS = 128
SLOTQ = 2
OWNB = 3
NRB = 16
NAUX = 8
NOB = 384
N_ORB = 32
DEVICES = 128


def owner_tables(key):
    order = jax.random.permutation(jax.random.fold_in(key, 11), NOB).astype(jnp.int32)
    inverse = jnp.argsort(order, stable=True).astype(jnp.int32)
    return (order, inverse)


def draw_block_owner(key, part):
    order, inverse = owner_tables(key)
    return jnp.stack([order // OWNB, order % OWNB], axis=1).astype(jnp.int32)


def draw_pair_map(key, part):
    order, inverse = owner_tables(key)
    key = jax.random.fold_in(key, 5)
    row_key, slot_key = jax.random.split(key)
    row_blocks = jax.random.randint(row_key, (N_ORB, DEVICES, SLOTQ), 0, NRB).astype(jnp.int32)
    local_slot = jax.random.randint(slot_key, (N_ORB, DEVICES, SLOTQ), 0, OWNB).astype(jnp.int32)
    owners = jnp.arange(DEVICES, dtype=jnp.int32)[None, :, None]
    orbital = inverse[owners * OWNB + local_slot]
    return jnp.stack([row_blocks, orbital], axis=3).astype(jnp.int32)


def draw_slot_counts(key, part):
    key = jax.random.fold_in(key, 7)
    count_key, full_key = jax.random.split(key)
    counts = jax.random.randint(count_key, (N_ORB, DEVICES), 1, SLOTQ + 1).astype(jnp.int32)
    full_owner = jax.random.randint(full_key, (), 0, DEVICES).astype(jnp.int32)
    owners = jnp.arange(DEVICES, dtype=jnp.int32)[None, :]
    return jnp.where(owners == full_owner, SLOTQ, counts).astype(jnp.int32)


def levels(own_key, dims, cuts, least, top_value):
    loudness = 1.0
    for dim, shards_of in cuts:
        heights = jax.random.uniform(jax.random.fold_in(jax.random.fold_in(own_key, 6), dim), (shards_of,), jnp.float32, least / len(cuts), top_value / len(cuts))
        loudness = loudness * jnp.repeat(jnp.exp(heights), dims[dim] // shards_of).reshape((-1,) + (1,) * (len(dims) - 1 - dim))
    return loudness


def bell_draw(key, extent, spread, limit, pieces=(), kind=jnp.bfloat16):
    array = spread * jax.random.normal(key, extent, jnp.float32)
    if pieces:
        array = array * levels(key, extent, pieces, -0.22, 0.18)
    return jnp.clip(array, -limit, limit).astype(kind)


def setup_inputs(seed: int = 0) -> dict:
    splits = jax.random.split(jax.random.key(seed), 6)
    return {
        "half_blocks": bell_draw(splits[0], (NAUX, N_ORB, DEVICES, SLOTQ, BS, OBS), 1.0, 6.0, ((0, 4), (1, 32))),
        "fit_coeffs": bell_draw(splits[1], (NAUX, NAUX), NAUX ** -0.5, 2.0),
        "pair_map": draw_pair_map(jax.random.fold_in(splits[5], 71), 0),
        "block_owner": draw_block_owner(jax.random.fold_in(splits[5], 71), 0),
        "slot_counts": draw_slot_counts(jax.random.fold_in(splits[5], 71), 0),
    }


def owner_term(half_blocks, fit_coeffs, pair_map, block_owner, slot_counts, device):
    blocks = lax.dynamic_index_in_dim(half_blocks, device, 2, keepdims=False).astype(jnp.float32)
    fitted = jnp.einsum('pq,qosxi->posxi', fit_coeffs.astype(jnp.float32), blocks).astype(jnp.bfloat16)
    counts = lax.dynamic_index_in_dim(slot_counts, device, 1, keepdims=False)
    slot_pairs = lax.dynamic_index_in_dim(pair_map, device, 1, keepdims=False)
    slot_ids = jnp.arange(SLOTQ, dtype=jnp.int32)
    live_mask = slot_ids[None, :] < counts[:, None]
    local_slot = block_owner[slot_pairs[:, :, 1], 1]
    column = local_slot * NRB + slot_pairs[:, :, 0]
    targets = jnp.arange(OWNB * NRB, dtype=jnp.int32)
    selector = ((column[:, :, None] == targets[None, None, :]) & live_mask[:, :, None]).astype(jnp.float32)
    gathered = jnp.einsum('osc,posxi->cxpi', selector, fitted.astype(jnp.float32)).astype(jnp.bfloat16)
    stacked = gathered.reshape(OWNB, NRB * BS, NAUX * OBS).astype(jnp.float32)
    return jnp.einsum('lak,lbk->ab', stacked, stacked)

def reference(half_blocks, fit_coeffs, pair_map, block_owner, slot_counts):

    def add_owner(device, running):
        return running + owner_term(half_blocks, fit_coeffs, pair_map, block_owner, slot_counts, device)
    start_sum = jnp.zeros((NRB * BS, NRB * BS), jnp.float32)
    running = lax.fori_loop(0, DEVICES, add_owner, start_sum)
    return running / math.sqrt(NOB * NAUX * OBS)
```

```python
import functools
import math

import jax
import jax.numpy as jnp
from jax import lax
from jax.experimental import pallas as pl
from jax.experimental.pallas import tpu as pltpu
from jax.sharding import PartitionSpec as P

MESH = pl.DeviceIdType.MESH
OWNB = 3
NRB = 16
MIB = 1 << 20

AXES = ((0, 1, 2), (1, 2, 0), (2, 0, 1))
UNITS = ((0, 0, 0, 80), (1, 0, 80, 96), (2, 0, 176, 80), (0, 1, 0, 96), (1, 1, 96, 80), (2, 1, 176, 80))


def place():
    a, o = lax.axis_index("aux"), lax.axis_index("orb")
    return a, o // 8, (o // 2) % 4, o % 2


def device(y, x, z, c):
    return (y, (x * 4 + z) * 2 + c)


def spread(units, h_ref, out_ref, b1_ref, b2_ref, s1, r1, s2, r2, s3, r3, l1, l3):
    me = place()

    def other(axis, k, dc=0):
        there = list(me)
        there[axis] = (me[axis] + k) % 4
        there[3] = (me[3] + dc) % 2
        return there

    barrier = pltpu.get_barrier_semaphore()
    mates = [other(axis, k, dc) for axis in range(3) for k in (1, 3, 2) for dc in (0, 1)] + [other(0, 0, 1)]
    for there in mates:
        pl.semaphore_signal(barrier, inc=1, device_id=device(*there), device_id_type=MESH)
    pl.semaphore_wait(barrier, len(mates))

    hops = [(1, 0), (3, 0), (2, 0), (1, 1), (3, 1), (2, 1), (0, 1)]

    def ways(u):
        g, q, row, n = units[u]
        return AXES[g] + (q, pl.ds(row, n))

    def at(ref, axes, index, q, rows, core=None):
        where = [slice(None)] * 4
        for axis, value in zip(axes, index):
            where[axis] = value
        if core is not None:
            where[3] = core
        return ref.at[tuple(where) + (q, rows)]

    def taken(axes, index, q, rows, core):
        where = [slice(None)] * 4
        for axis, value in zip(axes, index):
            where[axis] = value
        where[3] = core
        return h_ref.at[(q,) + tuple(where) + (rows,)]

    def remote(src, dst, send, recv, there):
        return pltpu.make_async_remote_copy(src, dst, send, recv, device_id=device(*there), device_id_type=MESH)

    def first_hop(u, j):
        A, B, C, q, rows = ways(u)
        there = other(A, *hops[j])
        return there, s1.at[u, j], r1.at[u, j]

    def start_first(u, j):
        A, B, C, q, rows = ways(u)
        there, send, recv = first_hop(u, j)
        for k in range(4):
            b = (me[B] + k) % 4
            ref = b1_ref if k else b2_ref
            remote(taken((A, B), (there[A], b), q, rows, there[3]), at(ref, (A, B), (me[A], b), q, rows, me[3]), send, recv, there).start()

    def whole_first(u, j):
        A, B, C, q, rows = ways(u)
        there, send, recv = first_hop(u, j)
        return remote(taken((A,), (there[A],), q, rows, there[3]), at(b1_ref, (A,), (me[A],), q, rows, me[3]), send, recv, there)

    def start_own(u):
        A, B, C, q, rows = ways(u)
        for k in range(4):
            b = (me[B] + k) % 4
            ref = b1_ref if k else b2_ref
            pltpu.make_async_copy(taken((A, B), (me[A], b), q, rows, me[3]), at(ref, (A, B), (me[A], b), q, rows, me[3]), l1.at[u]).start()

    def whole_own(u):
        A, B, C, q, rows = ways(u)
        return pltpu.make_async_copy(taken((A,), (me[A],), q, rows, me[3]), at(b1_ref, (A,), (me[A],), q, rows, me[3]), l1.at[u])

    turns = (1, 3, 2)

    def start_second(u, j):
        A, B, C, q, rows = ways(u)
        there = other(B, turns[j])
        for k in range(4):
            c = (me[C] + k) % 4
            ref = b2_ref if k else out_ref
            remote(at(b1_ref, (B, C), (there[B], c), q, rows), at(ref, (B, C), (me[B], c), q, rows), s2.at[u, j], r2.at[u, j], there).start()

    def whole_second(u, j):
        A, B, C, q, rows = ways(u)
        there = other(B, turns[j])
        return remote(at(b1_ref, (B,), (there[B],), q, rows), at(b2_ref, (B,), (me[B],), q, rows), s2.at[u, j], r2.at[u, j], there)

    def kept(u):
        A, B, C, q, rows = ways(u)
        return pltpu.make_async_copy(at(b2_ref, (B, C), (me[B], me[C]), q, rows), at(out_ref, (B, C), (me[B], me[C]), q, rows), l3.at[u])

    def third(u, j):
        A, B, C, q, rows = ways(u)
        there = other(C, turns[j])
        return remote(at(b2_ref, (C,), (there[C],), q, rows), at(out_ref, (C,), (me[C],), q, rows), s3.at[u, j], r3.at[u, j], there)

    n = len(units)
    waves = [list(range(i, min(i + 3, n))) for i in range(0, n, 3)]
    for us in waves:
        for j in range(7):
            for u in us:
                start_first(u, j)
        for u in us:
            start_own(u)
    for us in waves:
        for u in us:
            for j in range(7):
                whole_first(u, j).wait_recv()
            whole_own(u).wait()
        for j in range(3):
            for u in us:
                start_second(u, j)
        for u in us:
            kept(u).start()
    for us in waves:
        for u in us:
            for j in range(3):
                whole_second(u, j).wait_recv()
        for j in range(3):
            for u in us:
                third(u, j).start()
    for us in waves:
        for u in us:
            for j in range(3):
                third(u, j).wait_recv()
            kept(u).wait()
    for u in range(n):
        for j in range(7):
            whole_first(u, j).wait_send()
        for j in range(3):
            whole_second(u, j).wait_send()
            third(u, j).wait_send()


def all_to_all(h, units=UNITS):
    h = h.reshape(2, 4, 4, 4, 2, 256, 128)
    shape = jax.ShapeDtypeStruct((4, 4, 4, 2, 2, 256, 128), jnp.bfloat16)
    n = len(units)
    dma = pltpu.SemaphoreType.DMA
    out, _, _ = pl.pallas_call(
        functools.partial(spread, units),
        out_shape=(shape,) * 3,
        in_specs=[pl.BlockSpec(memory_space=pl.ANY)],
        out_specs=(pl.BlockSpec(memory_space=pl.ANY),) * 3,
        scratch_shapes=[dma((n, 7)), dma((n, 7)), dma((n, 3)), dma((n, 3)), dma((n, 3)), dma((n, 3)), dma((n,)), dma((n,))],
        compiler_params=pltpu.CompilerParams(collective_id=0, has_side_effects=True),
    )(h)
    return out


def fit(column, w_ref, r_ref, g_ref, head, chain, slots, acc, sems):
    target = pl.program_id(0)

    def block(slot):
        return pltpu.make_async_copy(r_ref.at[:, slot // 2, :, slot % 2], slots.at[slot], sems.at[slot])

    @pl.when(target == 0)
    def _():
        def clear(t, _):
            head[t] = -1
            return 0

        def link(slot, _):
            t = column[slot]
            chain[slot] = head[t]
            head[t] = slot
            return 0

        def load(t, _):
            def step(slot):
                block(slot).start()
                return chain[slot]

            lax.while_loop(lambda slot: slot >= 0, step, head[t])
            return 0

        lax.fori_loop(0, OWNB * NRB + 1, clear, 0)
        lax.fori_loop(0, 64, link, 0)
        lax.fori_loop(0, OWNB * NRB, load, 0)

    acc[...] = jnp.zeros_like(acc)

    def add(slot):
        block(slot).wait()
        stack = jnp.concatenate(
            [
                jnp.concatenate([slots[slot, a, q, pl.ds(32 * j, 32), :] for a in range(4) for q in range(2)], axis=0)
                for j in range(4)
            ],
            axis=1,
        )
        acc[...] += jnp.dot(w_ref[...], stack, preferred_element_type=jnp.float32).astype(jnp.bfloat16).astype(jnp.float32)
        return chain[slot]

    lax.while_loop(lambda slot: slot >= 0, add, head[target])
    for p in range(8):
        for j in range(4):
            g_ref[0, pl.ds(32 * j, 32), pl.ds(128 * p, 128)] = acc[pl.ds(32 * p, 32), pl.ds(128 * j, 128)].astype(jnp.bfloat16)


def gather_fit(received, fit_coeffs, pair_map, block_owner, slot_counts):
    owner = lax.axis_index("aux") * 32 + lax.axis_index("orb")
    counts = lax.dynamic_index_in_dim(slot_counts, owner, 1, keepdims=False)
    pairs = lax.dynamic_index_in_dim(pair_map, owner, 1, keepdims=False)
    live = jnp.arange(2, dtype=jnp.int32)[None, :] < counts[:, None]
    column = block_owner[pairs[:, :, 1], 1] * NRB + pairs[:, :, 0]
    column = jnp.where(live, column, OWNB * NRB).reshape(64)
    weights = jnp.kron(fit_coeffs, jnp.eye(32, dtype=jnp.bfloat16))
    smem = pltpu.SMEM
    return pl.pallas_call(
        fit,
        grid=(OWNB * NRB,),
        out_shape=jax.ShapeDtypeStruct((OWNB * NRB, 128, 1024), jnp.bfloat16),
        in_specs=[
            pl.BlockSpec(memory_space=smem),
            pl.BlockSpec((256, 256), lambda t: (0, 0)),
            pl.BlockSpec(memory_space=pl.ANY),
        ],
        out_specs=pl.BlockSpec((1, 128, 1024), lambda t: (t, 0, 0)),
        scratch_shapes=[
            smem((OWNB * NRB + 1,), jnp.int32),
            smem((64,), jnp.int32),
            pltpu.VMEM((64, 4, 2, 128, 128), jnp.bfloat16),
            pltpu.VMEM((256, 512), jnp.float32),
            pltpu.SemaphoreType.DMA((64,)),
        ],
        compiler_params=pltpu.CompilerParams(vmem_limit_bytes=40 * MIB),
    )(column, weights, received)


CUT = ((0, 640), (640, 640), (1280, 768))


def total(factor, g_ref, out_ref, acc, core_out, core_in, held, wire, in1, t2, in2, t3, in3, cs, cr, s1, r1, s2, r2, s3, r3):
    me = place()
    y, x, z, c = me

    def other(axis, k):
        there = list(me)
        there[axis] = (me[axis] + k) % 4
        return device(*there)

    partner = device(y, x, z, 1 - c)
    barrier = pltpu.get_barrier_semaphore()
    mates = [partner] + [other(axis, k) for axis in range(3) for k in (1, 2, 3)]
    for there in mates:
        pl.semaphore_signal(barrier, inc=1, device_id=there, device_id_type=MESH)
    pl.semaphore_wait(barrier, len(mates))

    def remote(src, dst, send, recv, there):
        return pltpu.make_async_remote_copy(src, dst, send, recv, device_id=there, device_id_type=MESH)

    def rows_of(p):
        return (y + 1 + p // 2) % 4, (x // 2 + 1 + p) % 2

    def core_copy(p):
        return remote(core_out.at[p], core_in.at[p], cs.at[p], cr.at[p], partner)

    def form(p):
        ty, pair = rows_of(p)
        first = pl.multiple_of((ty * 4 + pair * 2) * 128, 256)

        @pl.loop(0, 4)
        def _(n):
            start = pl.multiple_of(n * 512, 512)
            part = jnp.zeros((256, 512), jnp.float32)
            for l in range(OWNB):
                part += lax.dot_general(
                    g_ref[l, pl.ds(first, 256), :], g_ref[l, pl.ds(start, 512), :],
                    (((1,), (1,)), ((), ())), preferred_element_type=jnp.float32)
            acc[:, pl.ds(start, 512)] = part

        for j in range(2):
            for k in range(4):
                base = j * 128 + k * 32
                gone = acc[pl.ds(pl.multiple_of(base + 16 * (1 - c), 16), 16), :]
                core_out[p, j, k] = gone.astype(jnp.bfloat16)
        core_copy(p).start()

    def keep(p):
        ty, pair = rows_of(p)
        core_copy(p).wait_recv()
        for j in range(2):
            for k in range(4):
                base = j * 128 + k * 32
                sum_ = acc[pl.ds(pl.multiple_of(base + 16 * c, 16), 16), :] + core_in[p, j, k].astype(jnp.float32)
                held[ty, pair * 2 + j, k] = sum_
                wire[ty, pair * 2 + j, k] = sum_.astype(jnp.bfloat16)
        if p < 6:
            k = p // 2 + 1
            cols = pl.ds(*CUT[0])
            remote(wire.at[ty, pl.ds(pair * 2, 2), :, :, cols], in1[0].at[k - 1, pl.ds(pair * 2, 2)],
                   s1.at[0, k - 1], r1.at[0, k - 1], other(0, k)).start()
        cols = pl.ds(*CUT[1])
        for j in range(2 if p % 2 == 0 else 1):
            tx = pair * 2 + j if p % 2 == 0 else x + 1 - 2 * (x % 2)
            k = (tx - x + 4) % 4
            remote(wire.at[ty, tx, :, :, cols], in1[1].at[k - 1, ty],
                   s1.at[1, k - 1], r1.at[1, k - 1], device(y, tx, z, c)).start()
        cols = pl.ds(*CUT[2])
        for k in (1, 3, 2):
            tz = (z + k) % 4
            remote(wire.at[ty, pl.ds(pair * 2, 2), tz, :, cols], in1[2].at[k - 1, ty, pl.ds(pair * 2, 2)],
                   s1.at[2, k - 1], r1.at[2, k - 1], other(2, k)).start()

    for p in range(8):
        form(p)
        keep(p)

    arrived1 = [remote(in1[g].at[k], in1[g].at[k], s1.at[g, k], r1.at[g, k], partner) for g in range(3) for k in range(3)]
    own1 = (
        lambda i: held[y, i, :, :, pl.ds(*CUT[0])],
        lambda i: held[i, x, :, :, pl.ds(*CUT[1])],
        lambda i: held[i, :, z, :, pl.ds(*CUT[2])],
    )
    go2 = (
        lambda k: (t2[0].at[(x + k) % 4], other(1, k)),
        lambda k: (t2[1].at[:, (z + k) % 4], other(2, k)),
        lambda k: (t2[2].at[(y + k) % 4], other(0, k)),
    )
    copies2 = []
    for g in range(3):
        for k in range(3):
            arrived1[g * 3 + k].wait_recv()
        for i in range(4):
            t2[g][i] = own1[g](i) + (in1[g][0, i].astype(jnp.float32) + in1[g][1, i].astype(jnp.float32)
                                     + in1[g][2, i].astype(jnp.float32))
        for k in (1, 3, 2):
            src, there = go2[g](k)
            copy = remote(src, in2[g].at[k - 1], s2.at[g, k - 1], r2.at[g, k - 1], there)
            copy.start()
            copies2.append(copy)
    own2 = (lambda: t2[0][x], lambda: t2[1][:, z], lambda: t2[2][y])
    go3 = (
        lambda k: (t3[0].at[(z + k) % 4], other(2, k)),
        lambda k: (t3[1].at[(y + k) % 4], other(0, k)),
        lambda k: (t3[2].at[(x + k) % 4], other(1, k)),
    )
    copies3 = []
    for g in range(3):
        for copy in copies2[3 * g:3 * g + 3]:
            copy.wait_recv()
        t3[g][...] = own2[g]() + (in2[g][0] + in2[g][1] + in2[g][2])
        for k in (1, 3, 2):
            src, there = go3[g](k)
            copy = remote(src, in3[g].at[k - 1], s3.at[g, k - 1], r3.at[g, k - 1], there)
            copy.start()
            copies3.append(copy)
    own3 = (lambda: t3[0][z], lambda: t3[1][y], lambda: t3[2][x])
    for g in range(3):
        for copy in copies3[3 * g:3 * g + 3]:
            copy.wait_recv()
        out_ref[:, pl.ds(*CUT[g])] = (own3[g]() + (in3[g][0] + in3[g][1] + in3[g][2])) * factor
    for p in range(8):
        core_copy(p).wait_send()
    for copy in arrived1 + copies2 + copies3:
        copy.wait_send()


def gram_sum(gathered, factor):
    f32, bf16 = jnp.float32, jnp.bfloat16
    dma = pltpu.SemaphoreType.DMA
    width = [n for _, n in CUT]

    def entry(g_ref, out_ref, acc, core_out, core_in, held, wire, *rest):
        bufs, sems = rest[:15], rest[15:]
        total(factor, g_ref, out_ref, acc, core_out, core_in, held, wire,
              bufs[0:3], bufs[3:6], bufs[6:9], bufs[9:12], bufs[12:15], *sems)

    return pl.pallas_call(
        entry,
        out_shape=jax.ShapeDtypeStruct((16, 2048), f32),
        in_specs=[pl.BlockSpec(memory_space=pltpu.VMEM)],
        out_specs=pl.BlockSpec(memory_space=pltpu.VMEM),
        scratch_shapes=[
            pltpu.VMEM((256, 2048), f32),
            pltpu.VMEM((8, 2, 4, 16, 2048), bf16),
            pltpu.VMEM((8, 2, 4, 16, 2048), bf16),
            pltpu.VMEM((4, 4, 4, 16, 2048), f32),
            pltpu.VMEM((4, 4, 4, 16, 2048), bf16),
        ]
        + [pltpu.VMEM((3, 4, 4, 16, n), bf16) for n in width]
        + [pltpu.VMEM((4, 4, 16, n), f32) for n in width]
        + [pltpu.VMEM((3, 4, 16, n), f32) for n in width]
        + [pltpu.VMEM((4, 16, n), f32) for n in width]
        + [pltpu.VMEM((3, 16, n), f32) for n in width]
        + [dma((8,)), dma((8,))] + [dma((3, 3)) for _ in range(6)],
        compiler_params=pltpu.CompilerParams(collective_id=1, has_side_effects=True, vmem_limit_bytes=56 * MIB),
    )(gathered)


def shards(half_blocks, fit_coeffs, pair_map, block_owner, slot_counts):
    received = all_to_all(half_blocks).reshape(4, 32, 2, 2, 128, 128)
    gathered = gather_fit(received, fit_coeffs, pair_map, block_owner, slot_counts)
    factor = 1.0 / math.sqrt(block_owner.shape[0] * fit_coeffs.shape[0] * half_blocks.shape[5])
    return gram_sum(gathered.reshape(OWNB, NRB * 128, 1024), factor)


def solution(mesh):
    return jax.shard_map(
        shards,
        mesh=mesh,
        in_specs=(P("aux", "orb", None, None, None, None), P(), P(), P(), P()),
        out_specs=P(("aux", "orb"), None),
        check_vma=False,
    )
```

```python
import functools
import math

import jax
import jax.numpy as jnp
from jax import lax
from jax.experimental import pallas as pl
from jax.experimental.pallas import tpu as pltpu
from jax.sharding import PartitionSpec as P

MESH = pl.DeviceIdType.MESH
OWNB = 3
NRB = 16
MIB = 1 << 20

AXES = ((0, 1, 2), (1, 2, 0), (2, 0, 1))
UNITS = ((0, 0, 0, 80), (1, 0, 80, 96), (2, 0, 176, 80), (0, 1, 0, 96), (1, 1, 96, 80), (2, 1, 176, 80))


def place():
    a, o = lax.axis_index("aux"), lax.axis_index("orb")
    return a, o // 8, (o // 2) % 4, o % 2


def device(y, x, z, c):
    return (y, (x * 4 + z) * 2 + c)


def spread(units, h_ref, pair_ref, local_ref, count_ref, out_ref, column, b1_ref, b2_ref, pairs, local, counts, ts, s1, r1, s2, r2, s3, r3, l1, l3):
    me = place()
    tables = [
        pltpu.make_async_copy(src, dst, ts.at[i])
        for i, (src, dst) in enumerate(((pair_ref, pairs), (local_ref, local), (count_ref, counts)))
    ]
    for copy in tables:
        copy.start()

    def other(axis, k, dc=0):
        there = list(me)
        there[axis] = (me[axis] + k) % 4
        there[3] = (me[3] + dc) % 2
        return there

    barrier = pltpu.get_barrier_semaphore()
    mates = [other(axis, k, dc) for axis in range(3) for k in (1, 3, 2) for dc in (0, 1)] + [other(0, 0, 1)]
    for there in mates:
        pl.semaphore_signal(barrier, inc=1, device_id=device(*there), device_id_type=MESH)
    pl.semaphore_wait(barrier, len(mates))

    hops = [(1, 0), (3, 0), (2, 0), (1, 1), (3, 1), (2, 1), (0, 1)]

    def ways(u):
        g, q, row, n = units[u]
        return AXES[g] + (q, pl.ds(row, n))

    def at(ref, axes, index, q, rows, core=None):
        where = [slice(None)] * 4
        for axis, value in zip(axes, index):
            where[axis] = value
        if core is not None:
            where[3] = core
        return ref.at[tuple(where) + (q, rows)]

    def taken(axes, index, q, rows, core):
        where = [slice(None)] * 4
        for axis, value in zip(axes, index):
            where[axis] = value
        where[3] = core
        return h_ref.at[(q,) + tuple(where) + (rows,)]

    def remote(src, dst, send, recv, there):
        return pltpu.make_async_remote_copy(src, dst, send, recv, device_id=device(*there), device_id_type=MESH)

    def first_hop(u, j):
        A, B, C, q, rows = ways(u)
        there = other(A, *hops[j])
        return there, s1.at[u, j], r1.at[u, j]

    def start_first(u, j):
        A, B, C, q, rows = ways(u)
        there, send, recv = first_hop(u, j)
        for k in range(4):
            b = (me[B] + k) % 4
            ref = b1_ref if k else b2_ref
            remote(taken((A, B), (there[A], b), q, rows, there[3]), at(ref, (A, B), (me[A], b), q, rows, me[3]), send, recv, there).start()

    def whole_first(u, j):
        A, B, C, q, rows = ways(u)
        there, send, recv = first_hop(u, j)
        return remote(taken((A,), (there[A],), q, rows, there[3]), at(b1_ref, (A,), (me[A],), q, rows, me[3]), send, recv, there)

    def start_own(u):
        A, B, C, q, rows = ways(u)
        for k in range(4):
            b = (me[B] + k) % 4
            ref = b1_ref if k else b2_ref
            pltpu.make_async_copy(taken((A, B), (me[A], b), q, rows, me[3]), at(ref, (A, B), (me[A], b), q, rows, me[3]), l1.at[u]).start()

    def whole_own(u):
        A, B, C, q, rows = ways(u)
        return pltpu.make_async_copy(taken((A,), (me[A],), q, rows, me[3]), at(b1_ref, (A,), (me[A],), q, rows, me[3]), l1.at[u])

    turns = (1, 3, 2)

    def start_second(u, j):
        A, B, C, q, rows = ways(u)
        there = other(B, turns[j])
        for k in range(4):
            c = (me[C] + k) % 4
            ref = b2_ref if k else out_ref
            remote(at(b1_ref, (B, C), (there[B], c), q, rows), at(ref, (B, C), (me[B], c), q, rows), s2.at[u, j], r2.at[u, j], there).start()

    def whole_second(u, j):
        A, B, C, q, rows = ways(u)
        there = other(B, turns[j])
        return remote(at(b1_ref, (B,), (there[B],), q, rows), at(b2_ref, (B,), (me[B],), q, rows), s2.at[u, j], r2.at[u, j], there)

    def kept(u):
        A, B, C, q, rows = ways(u)
        return pltpu.make_async_copy(at(b2_ref, (B, C), (me[B], me[C]), q, rows), at(out_ref, (B, C), (me[B], me[C]), q, rows), l3.at[u])

    def third(u, j):
        A, B, C, q, rows = ways(u)
        there = other(C, turns[j])
        return remote(at(b2_ref, (C,), (there[C],), q, rows), at(out_ref, (C,), (me[C],), q, rows), s3.at[u, j], r3.at[u, j], there)

    n = len(units)
    waves = [list(range(i, min(i + 3, n))) for i in range(0, n, 3)]
    for us in waves:
        for j in range(7):
            for u in us:
                start_first(u, j)
        for u in us:
            start_own(u)
    for copy in tables:
        copy.wait()
    owner = (me[0] * 16 + me[1] * 4 + me[2]) * 2 + me[3]

    def target(slot, _):
        o, s = slot // 2, slot % 2
        t = local[1, pairs[o, s, 1, owner]] * NRB + pairs[o, s, 0, owner]
        column[slot] = jnp.where(s < counts[o, owner], t, OWNB * NRB)
        return 0

    lax.fori_loop(0, 64, target, 0)
    for us in waves:
        for u in us:
            for j in range(7):
                whole_first(u, j).wait_recv()
            whole_own(u).wait()
        for j in range(3):
            for u in us:
                start_second(u, j)
        for u in us:
            kept(u).start()
    for us in waves:
        for u in us:
            for j in range(3):
                whole_second(u, j).wait_recv()
        for j in range(3):
            for u in us:
                third(u, j).start()
    for us in waves:
        for u in us:
            for j in range(3):
                third(u, j).wait_recv()
            kept(u).wait()
    for u in range(n):
        for j in range(7):
            whole_first(u, j).wait_send()
        for j in range(3):
            whole_second(u, j).wait_send()
            third(u, j).wait_send()


def all_to_all(h, pair_map, block_owner, slot_counts, units=UNITS):
    h = h.reshape(2, 4, 4, 4, 2, 256, 128)
    pairs, local = jnp.transpose(pair_map, (0, 2, 3, 1)), jnp.transpose(block_owner)
    shape = jax.ShapeDtypeStruct((4, 4, 4, 2, 2, 256, 128), jnp.bfloat16)
    n = len(units)
    dma, smem = pltpu.SemaphoreType.DMA, pltpu.SMEM
    hbm = pl.BlockSpec(memory_space=pltpu.HBM)
    out, column, _, _ = pl.pallas_call(
        functools.partial(spread, units),
        out_shape=(shape, jax.ShapeDtypeStruct((64,), jnp.int32), shape, shape),
        in_specs=[hbm] * 4,
        out_specs=(hbm, pl.BlockSpec(memory_space=smem), hbm, hbm),
        scratch_shapes=[smem(pairs.shape, jnp.int32), smem(local.shape, jnp.int32), smem(slot_counts.shape, jnp.int32), dma((3,)),
                        dma((n, 7)), dma((n, 7)), dma((n, 3)), dma((n, 3)), dma((n, 3)), dma((n, 3)), dma((n,)), dma((n,))],
        compiler_params=pltpu.CompilerParams(collective_id=0, has_side_effects=True),
    )(h, pairs, local, slot_counts)
    return out, column


def fit(column, w_ref, r_ref, out_ref, head, chain, slots, g_ref, acc, sems, gone):
    def block(slot):
        return pltpu.make_async_copy(r_ref.at[:, slot // 2, :, slot % 2], slots.at[slot], sems.at[slot])

    def clear(t, _):
        head[t] = -1
        return 0

    def link(slot, _):
        t = column[slot]
        chain[slot] = head[t]
        head[t] = slot
        return 0

    def load(t, _):
        def begin(slot):
            block(slot).start()
            return chain[slot]

        lax.while_loop(lambda slot: slot >= 0, begin, head[t])
        return 0

    lax.fori_loop(0, OWNB * NRB + 1, clear, 0)
    lax.fori_loop(0, 64, link, 0)
    lax.fori_loop(0, OWNB * NRB, load, 0)

    def fitted(slot, j):
        stack = jnp.concatenate(
            [
                jnp.concatenate([slots[slot, a, q, pl.ds(32 * i, 32), :] for a in range(4) for q in range(2)], axis=0)
                for i in (2 * j, 2 * j + 1)
            ],
            axis=1,
        )
        return jnp.dot(w_ref[...], stack, preferred_element_type=jnp.float32).astype(jnp.bfloat16)

    def place_in(row, col, j, value):
        for p in range(8):
            for i in range(2):
                g_ref[pl.ds(row + 64 * j + 32 * i, 32), pl.ds(pl.multiple_of(col + 128 * p, 128), 128)] = value[32 * p:32 * p + 32, 128 * i:128 * i + 128]

    def pair(target, _):
        row = pl.multiple_of(target % NRB * 128, 128)
        col = pl.multiple_of(target // NRB * 1024, 1024)
        first = head[target]

        @pl.when(first < 0)
        def _():
            g_ref[pl.ds(row, 128), pl.ds(col, 1024)] = jnp.zeros((128, 1024), jnp.bfloat16)

        @pl.when(first >= 0)
        def _():
            block(first).wait()
            second = chain[first]

            @pl.when(second < 0)
            def _():
                for j in range(2):
                    place_in(row, col, j, fitted(first, j))

            @pl.when(second >= 0)
            def _():
                for j in range(2):
                    acc[j] = fitted(first, j).astype(jnp.float32)

                def add(slot):
                    block(slot).wait()
                    for j in range(2):
                        acc[j] += fitted(slot, j).astype(jnp.float32)
                    return chain[slot]

                lax.while_loop(lambda slot: slot >= 0, add, second)
                for j in range(2):
                    place_in(row, col, j, acc[j].astype(jnp.bfloat16))

        there = (pl.ds(row, 128), pl.ds(col, 1024))
        pltpu.make_async_copy(g_ref.at[there], out_ref.at[there], gone).start()
        return 0

    lax.fori_loop(0, OWNB * NRB, pair, 0)
    pltpu.make_async_copy(g_ref, out_ref, gone).wait()


def gather_fit(received, column, fit_coeffs):
    weights = jnp.kron(fit_coeffs, jnp.eye(32, dtype=jnp.bfloat16))
    smem = pltpu.SMEM
    return pl.pallas_call(
        fit,
        out_shape=jax.ShapeDtypeStruct((NRB * 128, OWNB * 1024), jnp.bfloat16),
        in_specs=[
            pl.BlockSpec(memory_space=smem),
            pl.BlockSpec(memory_space=pltpu.VMEM),
            pl.BlockSpec(memory_space=pltpu.HBM),
        ],
        out_specs=pl.BlockSpec(memory_space=pltpu.HBM),
        scratch_shapes=[
            smem((OWNB * NRB + 1,), jnp.int32),
            smem((64,), jnp.int32),
            pltpu.VMEM((64, 4, 2, 128, 128), jnp.bfloat16),
            pltpu.VMEM((NRB * 128, OWNB * 1024), jnp.bfloat16),
            pltpu.VMEM((2, 256, 256), jnp.float32),
            pltpu.SemaphoreType.DMA((64,)),
            pltpu.SemaphoreType.DMA,
        ],
        compiler_params=pltpu.CompilerParams(vmem_limit_bytes=58 * MIB),
    )(column, weights, received)


CUT = ((0, 640), (640, 640), (1280, 768))


def total(factor, g_ref, out_ref, g, acc, core_out, core_in, wire, in1, t2, in2, t3, in3, gs, cs, cr, s1, r1, s2, r2, s3, r3):
    me = place()
    y, x, z, c = me

    def other(axis, k):
        there = list(me)
        there[axis] = (me[axis] + k) % 4
        return device(*there)

    def remote(src, dst, send, recv, there):
        return pltpu.make_async_remote_copy(src, dst, send, recv, device_id=there, device_id_type=MESH)

    def rows_of(p):
        return (y + 1 + p // 2) % 4, (x // 2 + 1 + p) % 2

    def first_row(p):
        ty, pair = rows_of(p)
        return pl.multiple_of((ty * 4 + pair * 2) * 128, 256)

    def load(p):
        return pltpu.make_async_copy(g_ref.at[pl.ds(first_row(p), 256)], g.at[pl.ds(256 * p, 256)], gs.at[p])

    for p in range(8):
        load(p).start()
    partner = device(y, x, z, 1 - c)
    barrier = pltpu.get_barrier_semaphore()
    mates = [partner] + [other(axis, k) for axis in range(3) for k in (1, 2, 3)]
    for there in mates:
        pl.semaphore_signal(barrier, inc=1, device_id=there, device_id_type=MESH)
    pl.semaphore_wait(barrier, len(mates))

    def core_copy(p):
        return remote(core_out.at[p], core_in.at[p], cs.at[p], cr.at[p], partner)

    def form(p):
        here, mine = pl.ds(256 * p, 256), pl.ds(first_row(p), 256)

        def product(q):
            return lax.dot_general(
                g[here, :], g[256 * q:256 * q + 256, :], (((1,), (1,)), ((), ())), preferred_element_type=jnp.float32)

        @pl.when(c >= 0)
        def _():
            for q in range(p, 8):
                if p == 0:
                    load(q).wait()
                part = product(q)
                acc[here, pl.ds(first_row(q), 256)] = part
                if q > p:
                    acc[256 * q:256 * q + 256, mine] = part.T

        for j in range(2):
            for k in range(4):
                row = pl.multiple_of(256 * p + 128 * j + 32 * k + 16 * (1 - c), 16)
                core_out[p, j, k] = acc[pl.ds(row, 16), :].astype(jnp.bfloat16)
        core_copy(p).start()

    def pass_on(p):
        ty, pair = rows_of(p)
        core_copy(p).wait_recv()
        for j in range(2):
            for k in range(4):
                row = pl.multiple_of(256 * p + 128 * j + 32 * k + 16 * c, 16)
                wire[p, j, k] = (acc[pl.ds(row, 16), :] + core_in[p, j, k].astype(jnp.float32)).astype(jnp.bfloat16)
        if p < 6:
            k = p // 2 + 1
            remote(wire.at[p, :, :, :, pl.ds(*CUT[0])], in1[0].at[k - 1, pl.ds(pair * 2, 2)],
                   s1.at[0, k - 1], r1.at[0, k - 1], other(0, k)).start()
        for j in range(2 if p % 2 == 0 else 1):
            tx = pair * 2 + j if p % 2 == 0 else x + 1 - 2 * (x % 2)
            k = (tx - x + 4) % 4
            remote(wire.at[p, tx % 2, :, :, pl.ds(*CUT[1])], in1[1].at[k - 1, ty],
                   s1.at[1, k - 1], r1.at[1, k - 1], device(y, tx, z, c)).start()
        for k in (1, 3, 2):
            remote(wire.at[p, :, (z + k) % 4, :, pl.ds(*CUT[2])], in1[2].at[k - 1, ty, pl.ds(pair * 2, 2)],
                   s1.at[2, k - 1], r1.at[2, k - 1], other(2, k)).start()

    for p in range(8):
        form(p)
        if p:
            pass_on(p - 1)
    pass_on(7)

    def own(ty, tx, tz, cols):
        p = (ty - y + 3) % 4 * 2 + 1 - (tx // 2 + x // 2) % 2
        row = pl.multiple_of(256 * p + 128 * (tx % 2) + 32 * tz + 16 * c, 16)
        return acc[pl.ds(row, 16), pl.ds(*cols)] + core_in[p, tx % 2, tz, :, pl.ds(*cols)].astype(jnp.float32)

    arrived1 = [remote(in1[g].at[k], in1[g].at[k], s1.at[g, k], r1.at[g, k], partner) for g in range(3) for k in range(3)]
    own1 = (lambda i, j: own(y, i, j, CUT[0]), lambda i, j: own(i, x, j, CUT[1]), lambda i, j: own(i, j, z, CUT[2]))
    go2 = (
        lambda k: (t2[0].at[(x + k) % 4], other(1, k)),
        lambda k: (t2[1].at[:, (z + k) % 4], other(2, k)),
        lambda k: (t2[2].at[(y + k) % 4], other(0, k)),
    )
    copies2 = []
    for n in range(3):
        for k in range(3):
            arrived1[n * 3 + k].wait_recv()
        for i in range(4):
            for j in range(4):
                t2[n][i, j] = own1[n](i, j) + (in1[n][0, i, j].astype(jnp.float32) + in1[n][1, i, j].astype(jnp.float32)
                                               + in1[n][2, i, j].astype(jnp.float32))
        for k in (1, 3, 2):
            src, there = go2[n](k)
            copy = remote(src, in2[n].at[k - 1], s2.at[n, k - 1], r2.at[n, k - 1], there)
            copy.start()
            copies2.append(copy)
    own2 = (lambda: t2[0][x], lambda: t2[1][:, z], lambda: t2[2][y])
    go3 = (
        lambda k: (t3[0].at[(z + k) % 4], other(2, k)),
        lambda k: (t3[1].at[(y + k) % 4], other(0, k)),
        lambda k: (t3[2].at[(x + k) % 4], other(1, k)),
    )
    copies3 = []
    for n in range(3):
        for copy in copies2[3 * n:3 * n + 3]:
            copy.wait_recv()
        t3[n][...] = own2[n]() + (in2[n][0] + in2[n][1] + in2[n][2])
        for k in (1, 3, 2):
            src, there = go3[n](k)
            copy = remote(src, in3[n].at[k - 1], s3.at[n, k - 1], r3.at[n, k - 1], there)
            copy.start()
            copies3.append(copy)
    own3 = (lambda: t3[0][z], lambda: t3[1][y], lambda: t3[2][x])
    for n in range(3):
        for copy in copies3[3 * n:3 * n + 3]:
            copy.wait_recv()
        out_ref[:, pl.ds(*CUT[n])] = (own3[n]() + (in3[n][0] + in3[n][1] + in3[n][2])) * factor
    for p in range(8):
        core_copy(p).wait_send()
    for copy in arrived1 + copies2 + copies3:
        copy.wait_send()


def gram_sum(gathered, factor):
    f32, bf16 = jnp.float32, jnp.bfloat16
    dma = pltpu.SemaphoreType.DMA
    width = [n for _, n in CUT]

    def entry(g_ref, out_ref, g, acc, core_out, core_in, wire, *rest):
        bufs, sems = rest[:15], rest[15:]
        total(factor, g_ref, out_ref, g, acc, core_out, core_in, wire,
              bufs[0:3], bufs[3:6], bufs[6:9], bufs[9:12], bufs[12:15], *sems)

    return pl.pallas_call(
        entry,
        out_shape=jax.ShapeDtypeStruct((16, 2048), f32),
        in_specs=[pl.BlockSpec(memory_space=pltpu.HBM)],
        out_specs=pl.BlockSpec(memory_space=pltpu.VMEM),
        scratch_shapes=[
            pltpu.VMEM((2048, 3072), bf16),
            pltpu.VMEM((2048, 2048), f32),
            pltpu.VMEM((8, 2, 4, 16, 2048), bf16),
            pltpu.VMEM((8, 2, 4, 16, 2048), bf16),
            pltpu.VMEM((8, 2, 4, 16, 2048), bf16),
        ]
        + [pltpu.VMEM((3, 4, 4, 16, n), bf16) for n in width]
        + [pltpu.VMEM((4, 4, 16, n), f32) for n in width]
        + [pltpu.VMEM((3, 4, 16, n), f32) for n in width]
        + [pltpu.VMEM((4, 16, n), f32) for n in width]
        + [pltpu.VMEM((3, 16, n), f32) for n in width]
        + [dma((8,)), dma((8,)), dma((8,))] + [dma((3, 3)) for _ in range(6)],
        compiler_params=pltpu.CompilerParams(collective_id=1, has_side_effects=True, vmem_limit_bytes=58 * MIB),
    )(gathered)


def shards(half_blocks, fit_coeffs, pair_map, block_owner, slot_counts):
    received, column = all_to_all(half_blocks, pair_map, block_owner, slot_counts)
    gathered = gather_fit(received.reshape(4, 32, 2, 2, 128, 128), column, fit_coeffs)
    factor = 1.0 / math.sqrt(block_owner.shape[0] * fit_coeffs.shape[0] * half_blocks.shape[5])
    return gram_sum(gathered, factor)


def solution(mesh):
    return jax.shard_map(
        shards,
        mesh=mesh,
        in_specs=(P("aux", "orb", None, None, None, None), P(), P(), P(), P()),
        out_specs=P(("aux", "orb"), None),
        check_vma=False,
    )
```

```python
import functools
import math

import jax
import jax.numpy as jnp
from jax import lax
from jax.experimental import pallas as pl
from jax.experimental.pallas import tpu as pltpu
from jax.sharding import PartitionSpec as P

MESH = pl.DeviceIdType.MESH
OWNB = 3
NRB = 16
MIB = 1 << 20

AXES = ((0, 1, 2), (1, 2, 0), (2, 0, 1))
UNITS = (
    (0, 0, 0, 96), (1, 0, 96, 32), (1, 1, 0, 48), (2, 1, 48, 80),
    (0, 0, 128, 80), (1, 0, 208, 48), (1, 1, 128, 48), (2, 1, 176, 80),
)


def place():
    a, o = lax.axis_index("aux"), lax.axis_index("orb")
    return a, o // 8, (o // 2) % 4, o % 2


def device(y, x, z, c):
    return (y, (x * 4 + z) * 2 + c)


def fitted(w_ref, part, j):
    stack = jnp.concatenate(
        [jnp.concatenate([part(a, q, pl.ds(32 * i, 32)) for a in range(4) for q in range(2)], axis=0) for i in (2 * j, 2 * j + 1)],
        axis=1,
    )
    return jnp.dot(w_ref[...], stack, preferred_element_type=jnp.float32).astype(jnp.bfloat16)


def pieces(j, value):
    for p in range(8):
        for i in range(2):
            yield 64 * j + 32 * i, 128 * p, value[32 * p:32 * p + 32, 128 * i:128 * i + 128]


def spread(units, h_ref, c_ref, pair_ref, local_ref, count_ref, out_ref, ready_ref, column, w_ref, b1_ref, b2_ref, pairs, local, counts, raw, ready, ts, fs, s1, r1, s2, r2, s3, r3, l1, l3):
    me = place()
    tables = [
        pltpu.make_async_copy(src, dst, ts.at[i])
        for i, (src, dst) in enumerate(((pair_ref, pairs), (local_ref, local), (count_ref, counts)))
    ]
    for copy in tables:
        copy.start()

    def other(axis, k, dc=0):
        there = list(me)
        there[axis] = (me[axis] + k) % 4
        there[3] = (me[3] + dc) % 2
        return there

    barrier = pltpu.get_barrier_semaphore()
    mates = [other(axis, k, dc) for axis in range(3) for k in (1, 3, 2) for dc in (0, 1)] + [other(0, 0, 1)]
    for there in mates:
        pl.semaphore_signal(barrier, inc=1, device_id=device(*there), device_id_type=MESH)
    pl.semaphore_wait(barrier, len(mates))

    hops = [(1, 0), (3, 0), (2, 0), (1, 1), (3, 1), (2, 1), (0, 1)]

    def ways(u):
        g, q, row, n = units[u]
        return AXES[g] + (q, pl.ds(row, n))

    def at(ref, axes, index, q, rows, core=None):
        where = [slice(None)] * 4
        for axis, value in zip(axes, index):
            where[axis] = value
        if core is not None:
            where[3] = core
        return ref.at[tuple(where) + (q, rows)]

    def taken(axes, index, q, rows, core):
        where = [slice(None)] * 4
        for axis, value in zip(axes, index):
            where[axis] = value
        where[3] = core
        return h_ref.at[(q,) + tuple(where) + (rows,)]

    def remote(src, dst, send, recv, there):
        return pltpu.make_async_remote_copy(src, dst, send, recv, device_id=device(*there), device_id_type=MESH)

    def first_hop(u, j):
        A, B, C, q, rows = ways(u)
        there = other(A, *hops[j])
        return there, s1.at[u, j], r1.at[u, j]

    def start_first(u, j):
        A, B, C, q, rows = ways(u)
        there, send, recv = first_hop(u, j)
        for k in range(4):
            b = (me[B] + k) % 4
            ref = b1_ref if k else b2_ref
            remote(taken((A, B), (there[A], b), q, rows, there[3]), at(ref, (A, B), (me[A], b), q, rows, me[3]), send, recv, there).start()

    def whole_first(u, j):
        A, B, C, q, rows = ways(u)
        there, send, recv = first_hop(u, j)
        return remote(taken((A,), (there[A],), q, rows, there[3]), at(b1_ref, (A,), (me[A],), q, rows, me[3]), send, recv, there)

    def start_own(u):
        A, B, C, q, rows = ways(u)
        for k in range(4):
            b = (me[B] + k) % 4
            ref = b1_ref if k else b2_ref
            pltpu.make_async_copy(taken((A, B), (me[A], b), q, rows, me[3]), at(ref, (A, B), (me[A], b), q, rows, me[3]), l1.at[u]).start()

    def whole_own(u):
        A, B, C, q, rows = ways(u)
        return pltpu.make_async_copy(taken((A,), (me[A],), q, rows, me[3]), at(b1_ref, (A,), (me[A],), q, rows, me[3]), l1.at[u])

    turns = (1, 3, 2)

    def start_second(u, j):
        A, B, C, q, rows = ways(u)
        there = other(B, turns[j])
        for k in range(4):
            c = (me[C] + k) % 4
            ref = b2_ref if k else out_ref
            remote(at(b1_ref, (B, C), (there[B], c), q, rows), at(ref, (B, C), (me[B], c), q, rows), s2.at[u, j], r2.at[u, j], there).start()

    def whole_second(u, j):
        A, B, C, q, rows = ways(u)
        there = other(B, turns[j])
        return remote(at(b1_ref, (B,), (there[B],), q, rows), at(b2_ref, (B,), (me[B],), q, rows), s2.at[u, j], r2.at[u, j], there)

    def kept(u):
        A, B, C, q, rows = ways(u)
        return pltpu.make_async_copy(at(b2_ref, (B, C), (me[B], me[C]), q, rows), at(out_ref, (B, C), (me[B], me[C]), q, rows), l3.at[u])

    def third(u, j):
        A, B, C, q, rows = ways(u)
        there = other(C, turns[j])
        return remote(at(b2_ref, (C,), (there[C],), q, rows), at(out_ref, (C,), (me[C],), q, rows), s3.at[u, j], r3.at[u, j], there)

    n = len(units)
    waves = [list(range(n // 2)), list(range(n // 2, n))]
    for us in waves:
        for j in range(7):
            for u in us:
                start_first(u, j)
        for u in us:
            start_own(u)
    for copy in tables:
        copy.wait()
    owner = (me[0] * 16 + me[1] * 4 + me[2]) * 2 + me[3]

    def target(slot, _):
        o, s = slot // 2, slot % 2
        t = local[1, pairs[o, s, 1, owner]] * NRB + pairs[o, s, 0, owner]
        column[slot] = jnp.where(s < counts[o, owner], t, OWNB * NRB)
        return 0

    lax.fori_loop(0, 64, target, 0)

    wide = (lax.broadcasted_iota(jnp.int32, (256, 8), 0) // 32 == lax.broadcasted_iota(jnp.int32, (256, 8), 1)).astype(jnp.bfloat16)
    tall = jnp.dot(wide, c_ref[...], preferred_element_type=jnp.float32).astype(jnp.bfloat16)
    full = lax.dot_general(tall, wide, (((1,), (1,)), ((), ())), preferred_element_type=jnp.float32)
    row, col = (lax.broadcasted_iota(jnp.int32, (256, 256), i) % 32 for i in range(2))
    w_ref[...] = jnp.where(row == col, full, 0.0).astype(jnp.bfloat16)
    for us in waves:
        for u in us:
            for j in range(7):
                whole_first(u, j).wait_recv()
            whole_own(u).wait()
        for j in range(3):
            for u in us:
                start_second(u, j)
        for u in us:
            kept(u).start()
    for us in waves:
        for u in us:
            for j in range(3):
                whole_second(u, j).wait_recv()
        for j in range(3):
            for u in us:
                third(u, j).start()
    take = pltpu.make_async_copy(out_ref.at[:, :, :, :, :, pl.ds(0, 128)], raw, fs.at[0])
    give = pltpu.make_async_copy(ready, ready_ref, fs.at[1])

    def fit_first(o, _):
        for j in range(2):
            value = fitted(w_ref, lambda a, q, rows: raw[a, o // 8, o // 2 % 4, o % 2, q, rows, :], j)
            for row, col, piece in pieces(j, value):
                ready[o, row:row + 32, col:col + 128] = piece
        return 0

    for i, us in enumerate(waves):
        for u in us:
            for j in range(3):
                third(u, j).wait_recv()
            kept(u).wait()
        if i == 0:
            take.start()
            take.wait()
            lax.fori_loop(0, 32, fit_first, 0)
            give.start()
    give.wait()
    for u in range(n):
        for j in range(7):
            whole_first(u, j).wait_send()
        for j in range(3):
            whole_second(u, j).wait_send()
            third(u, j).wait_send()


def all_to_all(h, fit_coeffs, pair_map, block_owner, slot_counts, units=UNITS):
    h = h.reshape(2, 4, 4, 4, 2, 256, 128)
    pairs, local = jnp.transpose(pair_map, (0, 2, 3, 1)), jnp.transpose(block_owner)
    shape = jax.ShapeDtypeStruct((4, 4, 4, 2, 2, 256, 128), jnp.bfloat16)
    n = len(units)
    dma, smem = pltpu.SemaphoreType.DMA, pltpu.SMEM
    hbm = pl.BlockSpec(memory_space=pltpu.HBM)
    out, ready, column, weights, _, _ = pl.pallas_call(
        functools.partial(spread, units),
        out_shape=(shape, jax.ShapeDtypeStruct((32, 128, 1024), jnp.bfloat16), jax.ShapeDtypeStruct((64,), jnp.int32),
                   jax.ShapeDtypeStruct((256, 256), jnp.bfloat16), shape, shape),
        in_specs=[hbm, pl.BlockSpec(memory_space=pltpu.VMEM), hbm, hbm, hbm],
        out_specs=(hbm, hbm, pl.BlockSpec(memory_space=smem), pl.BlockSpec(memory_space=pltpu.VMEM), hbm, hbm),
        scratch_shapes=[smem(pairs.shape, jnp.int32), smem(local.shape, jnp.int32), smem(slot_counts.shape, jnp.int32),
                        pltpu.VMEM((4, 4, 4, 2, 2, 128, 128), jnp.bfloat16), pltpu.VMEM((32, 128, 1024), jnp.bfloat16),
                        dma((3,)), dma((2,)),
                        dma((n, 7)), dma((n, 7)), dma((n, 3)), dma((n, 3)), dma((n, 3)), dma((n, 3)), dma((n,)), dma((n,))],
        compiler_params=pltpu.CompilerParams(collective_id=0, has_side_effects=True, vmem_limit_bytes=58 * MIB),
    )(h, fit_coeffs, pairs, local, slot_counts)
    return out, ready, column, weights


def fit(column, w_ref, ready_ref, r_ref, out_ref, head, chain, slots, ready, g_ref, acc, sems, gone):
    def tile(target):
        return pl.ds(pl.multiple_of(target % NRB * 128, 128), 128), pl.ds(pl.multiple_of(target // NRB * 1024, 1024), 1024)

    def block(slot):
        return pltpu.make_async_copy(r_ref.at[:, slot // 2, :, 1], slots.at[slot // 2], sems.at[slot])

    def clear(t, _):
        head[t] = -1
        return 0

    def link(slot, _):
        t = column[slot]
        chain[slot] = head[t]
        head[t] = slot
        return 0

    def load(t, _):
        sole = jnp.logical_and(head[t] >= 0, chain[jnp.maximum(head[t], 0)] < 0)

        def begin(slot):
            first = slot % 2 == 0

            @pl.when(jnp.logical_and(first, sole))
            def _():
                pltpu.make_async_copy(ready_ref.at[slot // 2], g_ref.at[tile(t)], sems.at[slot]).start()

            @pl.when(jnp.logical_and(first, jnp.logical_not(sole)))
            def _():
                pltpu.make_async_copy(ready_ref.at[slot // 2], ready.at[slot // 2], sems.at[slot]).start()

            return chain[slot]

        lax.while_loop(lambda slot: slot >= 0, begin, head[t])
        return 0

    def early(o, _):
        @pl.when(column[2 * o + 1] < OWNB * NRB)
        def _():
            block(2 * o + 1).start()

        return 0

    lax.fori_loop(0, 32, early, 0)
    lax.fori_loop(0, OWNB * NRB + 1, clear, 0)
    lax.fori_loop(0, 64, link, 0)
    lax.fori_loop(0, OWNB * NRB, load, 0)

    def late(slot, j):
        return fitted(w_ref, lambda a, q, rows: slots[slot // 2, a, q, rows, :], j)

    def pair(target, _):
        row = pl.multiple_of(target % NRB * 128, 128)
        col = pl.multiple_of(target // NRB * 1024, 1024)
        first = head[target]
        second = chain[jnp.maximum(first, 0)]

        @pl.when(first < 0)
        def _():
            g_ref[tile(target)] = jnp.zeros((128, 1024), jnp.bfloat16)

        @pl.when(jnp.logical_and(first >= 0, second < 0))
        def _():
            block(first).wait()

            @pl.when(first % 2 == 1)
            def _():
                for j in range(2):
                    for r, k, piece in pieces(j, late(first, j)):
                        g_ref[pl.ds(row + r, 32), pl.ds(pl.multiple_of(col + k, 128), 128)] = piece

        @pl.when(jnp.logical_and(first >= 0, second >= 0))
        def _():
            acc[...] = jnp.zeros_like(acc)

            def add(slot):
                block(slot).wait()

                @pl.when(slot % 2 == 0)
                def _():
                    acc[...] += ready[slot // 2].astype(jnp.float32)

                @pl.when(slot % 2 == 1)
                def _():
                    for j in range(2):
                        for r, k, piece in pieces(j, late(slot, j)):
                            acc[r:r + 32, k:k + 128] += piece.astype(jnp.float32)

                return chain[slot]

            lax.while_loop(lambda slot: slot >= 0, add, first)
            g_ref[tile(target)] = acc[...].astype(jnp.bfloat16)

        pltpu.make_async_copy(g_ref.at[tile(target)], out_ref.at[tile(target)], gone).start()
        return 0

    lax.fori_loop(0, OWNB * NRB, pair, 0)
    pltpu.make_async_copy(g_ref, out_ref, gone).wait()


def gather_fit(received, ready, column, weights):
    smem = pltpu.SMEM
    return pl.pallas_call(
        fit,
        out_shape=jax.ShapeDtypeStruct((NRB * 128, OWNB * 1024), jnp.bfloat16),
        in_specs=[
            pl.BlockSpec(memory_space=smem),
            pl.BlockSpec(memory_space=pltpu.VMEM),
            pl.BlockSpec(memory_space=pltpu.HBM),
            pl.BlockSpec(memory_space=pltpu.HBM),
        ],
        out_specs=pl.BlockSpec(memory_space=pltpu.HBM),
        scratch_shapes=[
            smem((OWNB * NRB + 1,), jnp.int32),
            smem((64,), jnp.int32),
            pltpu.VMEM((32, 4, 2, 128, 128), jnp.bfloat16),
            pltpu.VMEM((32, 128, 1024), jnp.bfloat16),
            pltpu.VMEM((NRB * 128, OWNB * 1024), jnp.bfloat16),
            pltpu.VMEM((128, 1024), jnp.float32),
            pltpu.SemaphoreType.DMA((64,)),
            pltpu.SemaphoreType.DMA,
        ],
        compiler_params=pltpu.CompilerParams(vmem_limit_bytes=58 * MIB),
    )(column, weights, ready, received)


CUT = ((0, 640), (640, 640), (1280, 768))


def total(factor, g_ref, out_ref, g, acc, core_out, core_in, wire, in1, t2, in2, t3, in3, gs, cs, cr, s1, r1, s2, r2, s3, r3):
    me = place()
    y, x, z, c = me

    def other(axis, k):
        there = list(me)
        there[axis] = (me[axis] + k) % 4
        return device(*there)

    def remote(src, dst, send, recv, there):
        return pltpu.make_async_remote_copy(src, dst, send, recv, device_id=there, device_id_type=MESH)

    def rows_of(p):
        return (y + 1 + p // 2) % 4, (x // 2 + 1 + p) % 2

    def first_row(p):
        ty, pair = rows_of(p)
        return pl.multiple_of((ty * 4 + pair * 2) * 128, 256)

    def load(p):
        return pltpu.make_async_copy(g_ref.at[pl.ds(first_row(p), 256)], g.at[pl.ds(256 * p, 256)], gs.at[p])

    for p in range(8):
        load(p).start()
    partner = device(y, x, z, 1 - c)
    barrier = pltpu.get_barrier_semaphore()
    mates = [partner] + [other(axis, k) for axis in range(3) for k in (1, 2, 3)]
    for there in mates:
        pl.semaphore_signal(barrier, inc=1, device_id=there, device_id_type=MESH)
    pl.semaphore_wait(barrier, len(mates))

    def core_copy(p):
        return remote(core_out.at[p], core_in.at[p], cs.at[p], cr.at[p], partner)

    def form(p):
        here, mine = pl.ds(256 * p, 256), pl.ds(first_row(p), 256)

        def product(q):
            return lax.dot_general(
                g[here, :], g[256 * q:256 * q + 256, :], (((1,), (1,)), ((), ())), preferred_element_type=jnp.float32)

        @pl.when(c >= 0)
        def _():
            for q in range(p, 8):
                if p == 0:
                    load(q).wait()
                part = product(q)
                acc[here, pl.ds(first_row(q), 256)] = part
                if q > p:
                    acc[256 * q:256 * q + 256, mine] = part.T

        for j in range(2):
            for k in range(4):
                row = pl.multiple_of(256 * p + 128 * j + 32 * k + 16 * (1 - c), 16)
                core_out[p, j, k] = acc[pl.ds(row, 16), :].astype(jnp.bfloat16)
        core_copy(p).start()

    def pass_on(p):
        ty, pair = rows_of(p)
        core_copy(p).wait_recv()
        for j in range(2):
            for k in range(4):
                row = pl.multiple_of(256 * p + 128 * j + 32 * k + 16 * c, 16)
                wire[p, j, k] = (acc[pl.ds(row, 16), :] + core_in[p, j, k].astype(jnp.float32)).astype(jnp.bfloat16)
        if p < 6:
            k = p // 2 + 1
            remote(wire.at[p, :, :, :, pl.ds(*CUT[0])], in1[0].at[k - 1, pl.ds(pair * 2, 2)],
                   s1.at[0, k - 1], r1.at[0, k - 1], other(0, k)).start()
        for j in range(2 if p % 2 == 0 else 1):
            tx = pair * 2 + j if p % 2 == 0 else x + 1 - 2 * (x % 2)
            k = (tx - x + 4) % 4
            remote(wire.at[p, tx % 2, :, :, pl.ds(*CUT[1])], in1[1].at[k - 1, ty],
                   s1.at[1, k - 1], r1.at[1, k - 1], device(y, tx, z, c)).start()
        for k in (1, 3, 2):
            remote(wire.at[p, :, (z + k) % 4, :, pl.ds(*CUT[2])], in1[2].at[k - 1, ty, pl.ds(pair * 2, 2)],
                   s1.at[2, k - 1], r1.at[2, k - 1], other(2, k)).start()

    for p in range(8):
        form(p)
        if p:
            pass_on(p - 1)
    pass_on(7)

    def own(ty, tx, tz, cols):
        p = (ty - y + 3) % 4 * 2 + 1 - (tx // 2 + x // 2) % 2
        row = pl.multiple_of(256 * p + 128 * (tx % 2) + 32 * tz + 16 * c, 16)
        return acc[pl.ds(row, 16), pl.ds(*cols)] + core_in[p, tx % 2, tz, :, pl.ds(*cols)].astype(jnp.float32)

    arrived1 = [remote(in1[g].at[k], in1[g].at[k], s1.at[g, k], r1.at[g, k], partner) for g in range(3) for k in range(3)]
    own1 = (lambda i, j: own(y, i, j, CUT[0]), lambda i, j: own(i, x, j, CUT[1]), lambda i, j: own(i, j, z, CUT[2]))
    go2 = (
        lambda k: (t2[0].at[(x + k) % 4], other(1, k)),
        lambda k: (t2[1].at[:, (z + k) % 4], other(2, k)),
        lambda k: (t2[2].at[(y + k) % 4], other(0, k)),
    )
    copies2 = []
    for n in range(3):
        for k in range(3):
            arrived1[n * 3 + k].wait_recv()
        for i in range(4):
            for j in range(4):
                t2[n][i, j] = own1[n](i, j) + (in1[n][0, i, j].astype(jnp.float32) + in1[n][1, i, j].astype(jnp.float32)
                                               + in1[n][2, i, j].astype(jnp.float32))
        for k in (1, 3, 2):
            src, there = go2[n](k)
            copy = remote(src, in2[n].at[k - 1], s2.at[n, k - 1], r2.at[n, k - 1], there)
            copy.start()
            copies2.append(copy)
    own2 = (lambda: t2[0][x], lambda: t2[1][:, z], lambda: t2[2][y])
    go3 = (
        lambda k: (t3[0].at[(z + k) % 4], other(2, k)),
        lambda k: (t3[1].at[(y + k) % 4], other(0, k)),
        lambda k: (t3[2].at[(x + k) % 4], other(1, k)),
    )
    copies3 = []
    for n in range(3):
        for copy in copies2[3 * n:3 * n + 3]:
            copy.wait_recv()
        t3[n][...] = own2[n]() + (in2[n][0] + in2[n][1] + in2[n][2])
        for k in (1, 3, 2):
            src, there = go3[n](k)
            copy = remote(src, in3[n].at[k - 1], s3.at[n, k - 1], r3.at[n, k - 1], there)
            copy.start()
            copies3.append(copy)
    own3 = (lambda: t3[0][z], lambda: t3[1][y], lambda: t3[2][x])
    for n in range(3):
        for copy in copies3[3 * n:3 * n + 3]:
            copy.wait_recv()
        out_ref[:, pl.ds(*CUT[n])] = (own3[n]() + (in3[n][0] + in3[n][1] + in3[n][2])) * factor
    for p in range(8):
        core_copy(p).wait_send()
    for copy in arrived1 + copies2 + copies3:
        copy.wait_send()


def gram_sum(gathered, factor):
    f32, bf16 = jnp.float32, jnp.bfloat16
    dma = pltpu.SemaphoreType.DMA
    width = [n for _, n in CUT]

    def entry(g_ref, out_ref, g, acc, core_out, core_in, wire, *rest):
        bufs, sems = rest[:15], rest[15:]
        total(factor, g_ref, out_ref, g, acc, core_out, core_in, wire,
              bufs[0:3], bufs[3:6], bufs[6:9], bufs[9:12], bufs[12:15], *sems)

    return pl.pallas_call(
        entry,
        out_shape=jax.ShapeDtypeStruct((16, 2048), f32),
        in_specs=[pl.BlockSpec(memory_space=pltpu.HBM)],
        out_specs=pl.BlockSpec(memory_space=pltpu.VMEM),
        scratch_shapes=[
            pltpu.VMEM((2048, 3072), bf16),
            pltpu.VMEM((2048, 2048), f32),
            pltpu.VMEM((8, 2, 4, 16, 2048), bf16),
            pltpu.VMEM((8, 2, 4, 16, 2048), bf16),
            pltpu.VMEM((8, 2, 4, 16, 2048), bf16),
        ]
        + [pltpu.VMEM((3, 4, 4, 16, n), bf16) for n in width]
        + [pltpu.VMEM((4, 4, 16, n), f32) for n in width]
        + [pltpu.VMEM((3, 4, 16, n), f32) for n in width]
        + [pltpu.VMEM((4, 16, n), f32) for n in width]
        + [pltpu.VMEM((3, 16, n), f32) for n in width]
        + [dma((8,)), dma((8,)), dma((8,))] + [dma((3, 3)) for _ in range(6)],
        compiler_params=pltpu.CompilerParams(collective_id=1, has_side_effects=True, vmem_limit_bytes=58 * MIB),
    )(gathered)


def shards(half_blocks, fit_coeffs, pair_map, block_owner, slot_counts):
    received, ready, column, weights = all_to_all(half_blocks, fit_coeffs, pair_map, block_owner, slot_counts)
    gathered = gather_fit(received.reshape(4, 32, 2, 2, 128, 128), ready, column, weights)
    factor = 1.0 / math.sqrt(block_owner.shape[0] * fit_coeffs.shape[0] * half_blocks.shape[5])
    return gram_sum(gathered, factor)


def solution(mesh):
    return jax.shard_map(
        shards,
        mesh=mesh,
        in_specs=(P("aux", "orb", None, None, None, None), P(), P(), P(), P()),
        out_specs=P(("aux", "orb"), None),
        check_vma=False,
    )
```

```python
import functools
import math

import jax
import jax.numpy as jnp
from jax import lax
from jax.experimental import pallas as pl
from jax.experimental.pallas import tpu as pltpu
from jax.sharding import PartitionSpec as P

MESH = pl.DeviceIdType.MESH
OWNB = 3
NRB = 16
MIB = 1 << 20

AXES = ((0, 1, 2), (1, 2, 0), (2, 0, 1))
UNITS = (
    (0, 0, 0, 96), (1, 0, 96, 32), (1, 1, 0, 48), (2, 1, 48, 80),
    (0, 0, 128, 80), (1, 0, 208, 48), (1, 1, 128, 48), (2, 1, 176, 80),
)


def place():
    a, o = lax.axis_index("aux"), lax.axis_index("orb")
    return a, o // 8, (o // 2) % 4, o % 2


def device(y, x, z, c):
    return (y, (x * 4 + z) * 2 + c)


def fitted(w_ref, part, j):
    stack = jnp.concatenate(
        [jnp.concatenate([part(a, q, pl.ds(32 * i, 32)) for a in range(4) for q in range(2)], axis=0) for i in (2 * j, 2 * j + 1)],
        axis=1,
    )
    return jnp.dot(w_ref[...], stack, preferred_element_type=jnp.float32).astype(jnp.bfloat16)


def pieces(j, value):
    for p in range(8):
        for i in range(2):
            yield 64 * j + 32 * i, 128 * p, value[32 * p:32 * p + 32, 128 * i:128 * i + 128]


def spread(units, h_ref, c_ref, pair_ref, local_ref, count_ref, out_ref, ready_ref, column, w_ref, b1_ref, b2_ref, pairs, local, counts, raw, ready, ts, fs, s1, r1, s2, r2, s3, r3, l1, l3):
    me = place()
    tables = [
        pltpu.make_async_copy(src, dst, ts.at[i])
        for i, (src, dst) in enumerate(((pair_ref, pairs), (local_ref, local), (count_ref, counts)))
    ]
    for copy in tables:
        copy.start()

    def other(axis, k, dc=0):
        there = list(me)
        there[axis] = (me[axis] + k) % 4
        there[3] = (me[3] + dc) % 2
        return there

    barrier = pltpu.get_barrier_semaphore()
    mates = [other(axis, k, dc) for axis in range(3) for k in (1, 3, 2) for dc in (0, 1)] + [other(0, 0, 1)]
    for there in mates:
        pl.semaphore_signal(barrier, inc=1, device_id=device(*there), device_id_type=MESH)
    pl.semaphore_wait(barrier, len(mates))

    hops = [(1, 0), (3, 0), (2, 0), (1, 1), (3, 1), (2, 1), (0, 1)]

    def ways(u):
        g, q, row, n = units[u]
        return AXES[g] + (q, pl.ds(row, n))

    def at(ref, axes, index, q, rows, core=None):
        where = [slice(None)] * 4
        for axis, value in zip(axes, index):
            where[axis] = value
        if core is not None:
            where[3] = core
        return ref.at[tuple(where) + (q, rows)]

    def taken(axes, index, q, rows, core):
        where = [slice(None)] * 4
        for axis, value in zip(axes, index):
            where[axis] = value
        where[3] = core
        return h_ref.at[(q,) + tuple(where) + (rows,)]

    def remote(src, dst, send, recv, there):
        return pltpu.make_async_remote_copy(src, dst, send, recv, device_id=device(*there), device_id_type=MESH)

    def first_hop(u, j):
        A, B, C, q, rows = ways(u)
        there = other(A, *hops[j])
        return there, s1.at[u, j], r1.at[u, j]

    def start_first(u, j):
        A, B, C, q, rows = ways(u)
        there, send, recv = first_hop(u, j)
        for k in range(4):
            b = (me[B] + k) % 4
            ref = b1_ref if k else b2_ref
            remote(taken((A, B), (there[A], b), q, rows, there[3]), at(ref, (A, B), (me[A], b), q, rows, me[3]), send, recv, there).start()

    def whole_first(u, j):
        A, B, C, q, rows = ways(u)
        there, send, recv = first_hop(u, j)
        return remote(taken((A,), (there[A],), q, rows, there[3]), at(b1_ref, (A,), (me[A],), q, rows, me[3]), send, recv, there)

    def start_own(u):
        A, B, C, q, rows = ways(u)
        for k in range(4):
            b = (me[B] + k) % 4
            ref = b1_ref if k else b2_ref
            pltpu.make_async_copy(taken((A, B), (me[A], b), q, rows, me[3]), at(ref, (A, B), (me[A], b), q, rows, me[3]), l1.at[u]).start()

    def whole_own(u):
        A, B, C, q, rows = ways(u)
        return pltpu.make_async_copy(taken((A,), (me[A],), q, rows, me[3]), at(b1_ref, (A,), (me[A],), q, rows, me[3]), l1.at[u])

    turns = (1, 3, 2)

    def start_second(u, j):
        A, B, C, q, rows = ways(u)
        there = other(B, turns[j])
        for k in range(4):
            c = (me[C] + k) % 4
            ref = b2_ref if k else out_ref
            remote(at(b1_ref, (B, C), (there[B], c), q, rows), at(ref, (B, C), (me[B], c), q, rows), s2.at[u, j], r2.at[u, j], there).start()

    def whole_second(u, j):
        A, B, C, q, rows = ways(u)
        there = other(B, turns[j])
        return remote(at(b1_ref, (B,), (there[B],), q, rows), at(b2_ref, (B,), (me[B],), q, rows), s2.at[u, j], r2.at[u, j], there)

    def kept(u):
        A, B, C, q, rows = ways(u)
        return pltpu.make_async_copy(at(b2_ref, (B, C), (me[B], me[C]), q, rows), at(out_ref, (B, C), (me[B], me[C]), q, rows), l3.at[u])

    def third(u, j):
        A, B, C, q, rows = ways(u)
        there = other(C, turns[j])
        return remote(at(b2_ref, (C,), (there[C],), q, rows), at(out_ref, (C,), (me[C],), q, rows), s3.at[u, j], r3.at[u, j], there)

    n = len(units)
    waves = [list(range(n // 2)), list(range(n // 2, n))]
    for us in waves:
        for j in range(7):
            for u in us:
                start_first(u, j)
        for u in us:
            start_own(u)
    for copy in tables:
        copy.wait()
    owner = (me[0] * 16 + me[1] * 4 + me[2]) * 2 + me[3]

    def target(slot, _):
        o, s = slot // 2, slot % 2
        t = local[1, pairs[o, s, 1, owner]] * NRB + pairs[o, s, 0, owner]
        column[slot] = jnp.where(s < counts[o, owner], t, OWNB * NRB)
        return 0

    lax.fori_loop(0, 64, target, 0)

    wide = (lax.broadcasted_iota(jnp.int32, (256, 8), 0) // 32 == lax.broadcasted_iota(jnp.int32, (256, 8), 1)).astype(jnp.bfloat16)
    tall = jnp.dot(wide, c_ref[...], preferred_element_type=jnp.float32).astype(jnp.bfloat16)
    full = lax.dot_general(tall, wide, (((1,), (1,)), ((), ())), preferred_element_type=jnp.float32)
    row, col = (lax.broadcasted_iota(jnp.int32, (256, 256), i) % 32 for i in range(2))
    w_ref[...] = jnp.where(row == col, full, 0.0).astype(jnp.bfloat16)
    for us in waves:
        for u in us:
            for j in range(7):
                whole_first(u, j).wait_recv()
            whole_own(u).wait()
        for j in range(3):
            for u in us:
                start_second(u, j)
        for u in us:
            kept(u).start()
    for us in waves:
        for u in us:
            for j in range(3):
                whole_second(u, j).wait_recv()
        for j in range(3):
            for u in us:
                third(u, j).start()
    take = pltpu.make_async_copy(out_ref.at[:, :, :, :, :, pl.ds(0, 128)], raw, fs.at[0])
    give = pltpu.make_async_copy(ready, ready_ref, fs.at[1])

    def fit_first(o, _):
        for j in range(2):
            value = fitted(w_ref, lambda a, q, rows: raw[a, o // 8, o // 2 % 4, o % 2, q, rows, :], j)
            for row, col, piece in pieces(j, value):
                ready[o, row:row + 32, col:col + 128] = piece
        return 0

    for i, us in enumerate(waves):
        for u in us:
            for j in range(3):
                third(u, j).wait_recv()
            kept(u).wait()
        if i == 0:
            take.start()
            take.wait()
            lax.fori_loop(0, 32, fit_first, 0)
            give.start()
    give.wait()
    for u in range(n):
        for j in range(7):
            whole_first(u, j).wait_send()
        for j in range(3):
            whole_second(u, j).wait_send()
            third(u, j).wait_send()


def all_to_all(h, fit_coeffs, pair_map, block_owner, slot_counts, units=UNITS):
    h = h.reshape(2, 4, 4, 4, 2, 256, 128)
    pairs, local = jnp.transpose(pair_map, (0, 2, 3, 1)), jnp.transpose(block_owner)
    shape = jax.ShapeDtypeStruct((4, 4, 4, 2, 2, 256, 128), jnp.bfloat16)
    n = len(units)
    dma, smem = pltpu.SemaphoreType.DMA, pltpu.SMEM
    hbm = pl.BlockSpec(memory_space=pltpu.HBM)
    out, ready, column, weights, _, _ = pl.pallas_call(
        functools.partial(spread, units),
        out_shape=(shape, jax.ShapeDtypeStruct((32, 128, 1024), jnp.bfloat16), jax.ShapeDtypeStruct((64,), jnp.int32),
                   jax.ShapeDtypeStruct((256, 256), jnp.bfloat16), shape, shape),
        in_specs=[hbm, pl.BlockSpec(memory_space=pltpu.VMEM), hbm, hbm, hbm],
        out_specs=(hbm, hbm, pl.BlockSpec(memory_space=smem), pl.BlockSpec(memory_space=pltpu.VMEM), hbm, hbm),
        scratch_shapes=[smem(pairs.shape, jnp.int32), smem(local.shape, jnp.int32), smem(slot_counts.shape, jnp.int32),
                        pltpu.VMEM((4, 4, 4, 2, 2, 128, 128), jnp.bfloat16), pltpu.VMEM((32, 128, 1024), jnp.bfloat16),
                        dma((3,)), dma((2,)),
                        dma((n, 7)), dma((n, 7)), dma((n, 3)), dma((n, 3)), dma((n, 3)), dma((n, 3)), dma((n,)), dma((n,))],
        compiler_params=pltpu.CompilerParams(collective_id=0, has_side_effects=True, vmem_limit_bytes=58 * MIB),
    )(h, fit_coeffs, pairs, local, slot_counts)
    return out, ready, column, weights


def fit(column, w_ref, ready_ref, r_ref, out_ref, head, chain, slots, ready, g_ref, acc, sems, gone):
    def tile(target):
        return pl.ds(pl.multiple_of(target % NRB * 128, 128), 128), pl.ds(pl.multiple_of(target // NRB * 1024, 1024), 1024)

    def block(slot):
        return pltpu.make_async_copy(r_ref.at[:, slot // 2, :, 1], slots.at[slot // 2], sems.at[slot])

    def clear(t, _):
        head[t] = -1
        return 0

    def link(slot, _):
        t = column[slot]
        chain[slot] = head[t]
        head[t] = slot
        return 0

    def load(t, _):
        sole = jnp.logical_and(head[t] >= 0, chain[jnp.maximum(head[t], 0)] < 0)

        def begin(slot):
            first = slot % 2 == 0

            @pl.when(jnp.logical_and(first, sole))
            def _():
                pltpu.make_async_copy(ready_ref.at[slot // 2], g_ref.at[tile(t)], sems.at[slot]).start()

            @pl.when(jnp.logical_and(first, jnp.logical_not(sole)))
            def _():
                pltpu.make_async_copy(ready_ref.at[slot // 2], ready.at[slot // 2], sems.at[slot]).start()

            return chain[slot]

        lax.while_loop(lambda slot: slot >= 0, begin, head[t])
        return 0

    def early(o, _):
        @pl.when(column[2 * o + 1] < OWNB * NRB)
        def _():
            block(2 * o + 1).start()

        return 0

    lax.fori_loop(0, 32, early, 0)
    lax.fori_loop(0, OWNB * NRB + 1, clear, 0)
    lax.fori_loop(0, 64, link, 0)
    lax.fori_loop(0, OWNB * NRB, load, 0)

    def late(slot, j):
        return fitted(w_ref, lambda a, q, rows: slots[slot // 2, a, q, rows, :], j)

    def pair(target, _):
        row = pl.multiple_of(target % NRB * 128, 128)
        col = pl.multiple_of(target // NRB * 1024, 1024)
        first = head[target]
        second = chain[jnp.maximum(first, 0)]

        @pl.when(first < 0)
        def _():
            g_ref[tile(target)] = jnp.zeros((128, 1024), jnp.bfloat16)

        @pl.when(jnp.logical_and(first >= 0, second < 0))
        def _():
            block(first).wait()

            @pl.when(first % 2 == 1)
            def _():
                for j in range(2):
                    for r, k, piece in pieces(j, late(first, j)):
                        g_ref[pl.ds(row + r, 32), pl.ds(pl.multiple_of(col + k, 128), 128)] = piece

        @pl.when(jnp.logical_and(first >= 0, second >= 0))
        def _():
            block(first).wait()

            @pl.when(first % 2 == 0)
            def _():
                acc[...] = ready[first // 2].astype(jnp.float32)

            @pl.when(first % 2 == 1)
            def _():
                for j in range(2):
                    for r, k, piece in pieces(j, late(first, j)):
                        acc[r:r + 32, k:k + 128] = piece.astype(jnp.float32)

            def add(slot):
                block(slot).wait()

                @pl.when(slot % 2 == 0)
                def _():
                    acc[...] += ready[slot // 2].astype(jnp.float32)

                @pl.when(slot % 2 == 1)
                def _():
                    for j in range(2):
                        for r, k, piece in pieces(j, late(slot, j)):
                            acc[r:r + 32, k:k + 128] += piece.astype(jnp.float32)

                return chain[slot]

            lax.while_loop(lambda slot: slot >= 0, add, second)
            g_ref[tile(target)] = acc[...].astype(jnp.bfloat16)

        pltpu.make_async_copy(g_ref.at[tile(target)], out_ref.at[tile(target)], gone).start()
        return 0

    lax.fori_loop(0, OWNB * NRB, pair, 0)
    pltpu.make_async_copy(g_ref, out_ref, gone).wait()


def gather_fit(received, ready, column, weights):
    smem = pltpu.SMEM
    return pl.pallas_call(
        fit,
        out_shape=jax.ShapeDtypeStruct((NRB * 128, OWNB * 1024), jnp.bfloat16),
        in_specs=[
            pl.BlockSpec(memory_space=smem),
            pl.BlockSpec(memory_space=pltpu.VMEM),
            pl.BlockSpec(memory_space=pltpu.HBM),
            pl.BlockSpec(memory_space=pltpu.HBM),
        ],
        out_specs=pl.BlockSpec(memory_space=pltpu.HBM),
        scratch_shapes=[
            smem((OWNB * NRB + 1,), jnp.int32),
            smem((64,), jnp.int32),
            pltpu.VMEM((32, 4, 2, 128, 128), jnp.bfloat16),
            pltpu.VMEM((32, 128, 1024), jnp.bfloat16),
            pltpu.VMEM((NRB * 128, OWNB * 1024), jnp.bfloat16),
            pltpu.VMEM((128, 1024), jnp.float32),
            pltpu.SemaphoreType.DMA((64,)),
            pltpu.SemaphoreType.DMA,
        ],
        compiler_params=pltpu.CompilerParams(vmem_limit_bytes=58 * MIB),
    )(column, weights, ready, received)


CUT = ((0, 640), (640, 640), (1280, 768))


def total(factor, g_ref, out_ref, g, acc, core_out, core_in, wire, in1, t2, in2, t3, in3, gs, cs, cr, s1, r1, s2, r2, s3, r3):
    me = place()
    y, x, z, c = me

    def other(axis, k):
        there = list(me)
        there[axis] = (me[axis] + k) % 4
        return device(*there)

    def remote(src, dst, send, recv, there):
        return pltpu.make_async_remote_copy(src, dst, send, recv, device_id=there, device_id_type=MESH)

    def rows_of(p):
        return (y + 1 + p // 2) % 4, (x // 2 + 1 + p) % 2

    def first_row(p):
        ty, pair = rows_of(p)
        return pl.multiple_of((ty * 4 + pair * 2) * 128, 256)

    def load(p):
        return pltpu.make_async_copy(g_ref.at[pl.ds(first_row(p), 256)], g.at[pl.ds(256 * p, 256)], gs.at[p])

    for p in range(8):
        load(p).start()
    partner = device(y, x, z, 1 - c)
    barrier = pltpu.get_barrier_semaphore()
    mates = [partner] + [other(axis, k) for axis in range(3) for k in (1, 2, 3)]
    for there in mates:
        pl.semaphore_signal(barrier, inc=1, device_id=there, device_id_type=MESH)
    pl.semaphore_wait(barrier, len(mates))

    def core_copy(p):
        return remote(core_out.at[p], core_in.at[p], cs.at[p], cr.at[p], partner)

    def form(p):
        here, mine = pl.ds(256 * p, 256), pl.ds(first_row(p), 256)

        def product(q):
            return lax.dot_general(
                g[here, :], g[256 * q:256 * q + 256, :], (((1,), (1,)), ((), ())), preferred_element_type=jnp.float32)

        @pl.when(c >= 0)
        def _():
            for q in range(p, 8):
                if p == 0:
                    load(q).wait()
                part = product(q)
                acc[here, pl.ds(first_row(q), 256)] = part
                if q > p:
                    acc[256 * q:256 * q + 256, mine] = part.T

        for j in range(2):
            for k in range(4):
                row = pl.multiple_of(256 * p + 128 * j + 32 * k + 16 * (1 - c), 16)
                core_out[p, j, k] = acc[pl.ds(row, 16), :].astype(jnp.bfloat16)
        core_copy(p).start()

    def pass_on(p):
        ty, pair = rows_of(p)
        core_copy(p).wait_recv()
        for j in range(2):
            for k in range(4):
                row = pl.multiple_of(256 * p + 128 * j + 32 * k + 16 * c, 16)
                wire[p, j, k] = (acc[pl.ds(row, 16), :] + core_in[p, j, k].astype(jnp.float32)).astype(jnp.bfloat16)
        if p < 6:
            k = p // 2 + 1
            remote(wire.at[p, :, :, :, pl.ds(*CUT[0])], in1[0].at[k - 1, pl.ds(pair * 2, 2)],
                   s1.at[0, k - 1], r1.at[0, k - 1], other(0, k)).start()
        for j in range(2 if p % 2 == 0 else 1):
            tx = pair * 2 + j if p % 2 == 0 else x + 1 - 2 * (x % 2)
            k = (tx - x + 4) % 4
            remote(wire.at[p, tx % 2, :, :, pl.ds(*CUT[1])], in1[1].at[k - 1, ty],
                   s1.at[1, k - 1], r1.at[1, k - 1], device(y, tx, z, c)).start()
        for k in (1, 3, 2):
            remote(wire.at[p, :, (z + k) % 4, :, pl.ds(*CUT[2])], in1[2].at[k - 1, ty, pl.ds(pair * 2, 2)],
                   s1.at[2, k - 1], r1.at[2, k - 1], other(2, k)).start()

    for p in range(8):
        form(p)
        if p:
            pass_on(p - 1)
    pass_on(7)

    def own(ty, tx, tz, cols):
        p = (ty - y + 3) % 4 * 2 + 1 - (tx // 2 + x // 2) % 2
        row = pl.multiple_of(256 * p + 128 * (tx % 2) + 32 * tz + 16 * c, 16)
        return acc[pl.ds(row, 16), pl.ds(*cols)] + core_in[p, tx % 2, tz, :, pl.ds(*cols)].astype(jnp.float32)

    arrived1 = [remote(in1[g].at[k], in1[g].at[k], s1.at[g, k], r1.at[g, k], partner) for g in range(3) for k in range(3)]
    own1 = (lambda i, j: own(y, i, j, CUT[0]), lambda i, j: own(i, x, j, CUT[1]), lambda i, j: own(i, j, z, CUT[2]))
    go2 = (
        lambda k: (t2[0].at[(x + k) % 4], other(1, k)),
        lambda k: (t2[1].at[:, (z + k) % 4], other(2, k)),
        lambda k: (t2[2].at[(y + k) % 4], other(0, k)),
    )
    copies2 = []
    for n in range(3):
        for k in range(3):
            arrived1[n * 3 + k].wait_recv()
        for i in range(4):
            for j in range(4):
                t2[n][i, j] = own1[n](i, j) + (in1[n][0, i, j].astype(jnp.float32) + in1[n][1, i, j].astype(jnp.float32)
                                               + in1[n][2, i, j].astype(jnp.float32))
        for k in (1, 3, 2):
            src, there = go2[n](k)
            copy = remote(src, in2[n].at[k - 1], s2.at[n, k - 1], r2.at[n, k - 1], there)
            copy.start()
            copies2.append(copy)
    own2 = (lambda: t2[0][x], lambda: t2[1][:, z], lambda: t2[2][y])
    go3 = (
        lambda k: (t3[0].at[(z + k) % 4], other(2, k)),
        lambda k: (t3[1].at[(y + k) % 4], other(0, k)),
        lambda k: (t3[2].at[(x + k) % 4], other(1, k)),
    )
    copies3 = []
    for n in range(3):
        for copy in copies2[3 * n:3 * n + 3]:
            copy.wait_recv()
        t3[n][...] = own2[n]() + (in2[n][0] + in2[n][1] + in2[n][2])
        for k in (1, 3, 2):
            src, there = go3[n](k)
            copy = remote(src, in3[n].at[k - 1], s3.at[n, k - 1], r3.at[n, k - 1], there)
            copy.start()
            copies3.append(copy)
    own3 = (lambda: t3[0][z], lambda: t3[1][y], lambda: t3[2][x])
    for n in range(3):
        for copy in copies3[3 * n:3 * n + 3]:
            copy.wait_recv()
        out_ref[:, pl.ds(*CUT[n])] = (own3[n]() + (in3[n][0] + in3[n][1] + in3[n][2])) * factor
    for p in range(8):
        core_copy(p).wait_send()
    for copy in arrived1 + copies2 + copies3:
        copy.wait_send()


def gram_sum(gathered, factor):
    f32, bf16 = jnp.float32, jnp.bfloat16
    dma = pltpu.SemaphoreType.DMA
    width = [n for _, n in CUT]

    def entry(g_ref, out_ref, g, acc, core_out, core_in, wire, *rest):
        bufs, sems = rest[:15], rest[15:]
        total(factor, g_ref, out_ref, g, acc, core_out, core_in, wire,
              bufs[0:3], bufs[3:6], bufs[6:9], bufs[9:12], bufs[12:15], *sems)

    return pl.pallas_call(
        entry,
        out_shape=jax.ShapeDtypeStruct((16, 2048), f32),
        in_specs=[pl.BlockSpec(memory_space=pltpu.HBM)],
        out_specs=pl.BlockSpec(memory_space=pltpu.VMEM),
        scratch_shapes=[
            pltpu.VMEM((2048, 3072), bf16),
            pltpu.VMEM((2048, 2048), f32),
            pltpu.VMEM((8, 2, 4, 16, 2048), bf16),
            pltpu.VMEM((8, 2, 4, 16, 2048), bf16),
            pltpu.VMEM((8, 2, 4, 16, 2048), bf16),
        ]
        + [pltpu.VMEM((3, 4, 4, 16, n), bf16) for n in width]
        + [pltpu.VMEM((4, 4, 16, n), f32) for n in width]
        + [pltpu.VMEM((3, 4, 16, n), f32) for n in width]
        + [pltpu.VMEM((4, 16, n), f32) for n in width]
        + [pltpu.VMEM((3, 16, n), f32) for n in width]
        + [dma((8,)), dma((8,)), dma((8,))] + [dma((3, 3)) for _ in range(6)],
        compiler_params=pltpu.CompilerParams(collective_id=1, has_side_effects=True, vmem_limit_bytes=58 * MIB),
    )(gathered)


def shards(half_blocks, fit_coeffs, pair_map, block_owner, slot_counts):
    received, ready, column, weights = all_to_all(half_blocks, fit_coeffs, pair_map, block_owner, slot_counts)
    gathered = gather_fit(received.reshape(4, 32, 2, 2, 128, 128), ready, column, weights)
    factor = 1.0 / math.sqrt(block_owner.shape[0] * fit_coeffs.shape[0] * half_blocks.shape[5])
    return gram_sum(gathered, factor)


def solution(mesh):
    return jax.shard_map(
        shards,
        mesh=mesh,
        in_specs=(P("aux", "orb", None, None, None, None), P(), P(), P(), P()),
        out_specs=P(("aux", "orb"), None),
        check_vma=False,
    )
```
